512 devices in a mesh: group: 8 (over x, core), shard: 64 (over z, y).
Axes of the slice: x: 4, y: 8, z: 8, core: 2. Of those that a mesh axis runs over, the one named last changes fastest.
Arguments:
- queries: bfloat16 [4096, 768], P(('group', 'shard'))
- positives: int32 [4096], P(('group', 'shard')), may hold values from 0 to 196607
- cache: bfloat16 [196608, 768], P('shard')
- fresh: bfloat16 [8192, 768], P(('group', 'shard')), may hold values from -12 to 12
- slots: int32 [8192], P(('group', 'shard')), may hold values from 0 to 196607, as said below
Outputs:
- query_grad: float32 [4096, 768], P(('group', 'shard'))
- loss: float32 [4096], P(('group', 'shard'))
The draws below stay inside these ranges and needn't reach their ends.
Inputs may be any that keep to these rules, and one draw needn't show every extreme that they name: All 8192 slots are distinct; the fresh passage in row r has its slot among cache rows s * 3072 to (s + 1) * 3072 - 1, where s = (r // 16) % (the size of shard); in each such range rows s * 3072 and (s + 1) * 3072 - 1 are overwritten.
All inputs are finite; a program needn't handle non-finite values.
Results may differ from the reference program's by a relative error of at most 0.004.
Values may be sent and summed in bfloat16 or wider, within the bound.
No kernel may reach another device: no remote copies, remote signals or barrier semaphores. Data moves between devices by JAX's collectives and lax.ppermute only.
A program may use at most 128 MiB of HBM per device.

```python
import math
import jax
import jax.numpy as jnp
from jax import lax

D = 768
C_DEV = 3072
F_DEV = 16
GROUP_Q = 512
QUERIES = 4096
CACHE = 196608
FRESH = 8192
N_GROUP = 8
N_SHARD = 64


def cache_values(key):
    base = jax.random.normal(jax.random.fold_in(key, 101), (CACHE, D), jnp.float32)
    row_scale = jnp.exp(jax.random.uniform(jax.random.fold_in(key, 102), (CACHE, 1), jnp.float32, math.log(0.3), math.log(3.0)))
    return base * row_scale


def draw_cache(key, part):
    return cache_values(key).astype(jnp.bfloat16)


def draw_queries(key, part):
    key = jax.random.fold_in(key, 2)
    row_scale = jnp.exp(jax.random.uniform(jax.random.fold_in(key, 3), (QUERIES, 1), jnp.float32, math.log(0.5), math.log(2.0)))
    return (jax.random.normal(key, (QUERIES, D), jnp.float32) * row_scale).astype(jnp.bfloat16)


def shard_offsets(key_one):
    inner = jax.random.permutation(key_one, C_DEV - 2)[:N_GROUP * F_DEV - 2] + 1
    chosen = jnp.concatenate([jnp.array([0, C_DEV - 1], jnp.int32), inner.astype(jnp.int32)])
    return jax.random.permutation(jax.random.fold_in(key_one, 9), chosen)


def draw_slots(key, part):
    key = jax.random.fold_in(key, 5)
    shard_keys = jax.random.split(key, N_SHARD)
    offsets = jax.vmap(shard_offsets)(shard_keys)
    offsets = offsets.reshape(N_SHARD, N_GROUP, F_DEV).transpose(1, 0, 2)
    starts = (jnp.arange(N_SHARD, dtype=jnp.int32) * C_DEV)[None, :, None]
    return (offsets + starts).reshape(FRESH).astype(jnp.int32)


def with_ends(drawn, key, low, largest):
    dims = drawn.shape
    index_at = [jax.random.randint(jax.random.fold_in(key, axis), (), 0, dims[axis]) for axis in range(len(dims))]
    drawn = drawn.at[tuple(index_at)].set(low)
    longest = dims.index(max(dims))
    index_at[longest] = (index_at[longest] + 1) % dims[longest]
    return drawn.at[tuple(index_at)].set(largest)


def block_levels(stream_key, dims, pieces, least, top_value):
    def one(axis_at, blocks):
        steps = jax.random.uniform(jax.random.fold_in(jax.random.fold_in(stream_key, 6), axis_at), (blocks,), jnp.float32, least / len(pieces), top_value / len(pieces))
        return jnp.repeat(jnp.exp(steps), dims[axis_at] // blocks).reshape((-1,) + (1,) * (len(dims) - axis_at - 1))

    loudness = one(*pieces[0])
    for cut in pieces[1:]:
        loudness = loudness * one(*cut)
    return loudness


def noise(own_key, shape, deviation, limit, cuts=(), kind=jnp.bfloat16):
    values = deviation * jax.random.normal(own_key, shape, jnp.float32)
    if cuts:
        values = values * block_levels(own_key, shape, cuts, -0.22, 0.18)
    return jnp.clip(values, -limit, limit).astype(kind)


def setup_inputs(seed: int = 0) -> dict:
    arg_keys = jax.random.split(jax.random.key(seed), 6)
    queries = draw_queries(jax.random.fold_in(arg_keys[5], 71), 0)
    positives = with_ends(jax.random.randint(arg_keys[1], (QUERIES,), 0, CACHE), jax.random.fold_in(arg_keys[1], 1), 0, CACHE - 1).astype(jnp.int32)
    cache = draw_cache(jax.random.fold_in(arg_keys[5], 71), 0)
    fresh = noise(arg_keys[3], (FRESH, D), 2.0, 12.0, ((0, 512),))
    slots = draw_slots(jax.random.fold_in(arg_keys[5], 71), 0)
    return {"queries": queries, "positives": positives, "cache": cache, "fresh": fresh, "slots": slots}


def one_group(inputs, updated):
    group_rows, group_pos = inputs
    score_scale = 1.0 / jnp.sqrt(jnp.float32(D))
    scores = jnp.dot(group_rows, updated.T, preferred_element_type=jnp.float32) * score_scale
    row_top = lax.optimization_barrier(jnp.max(scores, axis=1))
    shifted = jnp.exp(scores - row_top[:, None])
    row_total = lax.optimization_barrier(jnp.sum(shifted, axis=1))
    pos_score = jnp.take_along_axis(scores, group_pos[:, None].astype(jnp.int32), axis=1)[:, 0]
    loss = jnp.log(row_total) + row_top - pos_score
    weights = (shifted / row_total[:, None]).astype(jnp.bfloat16)
    pos_rows = updated[group_pos].astype(jnp.float32)
    grads = (jnp.dot(weights, updated, preferred_element_type=jnp.float32) - pos_rows) * score_scale
    return (grads, loss)

def reference(queries, positives, cache, fresh, slots):
    updated = cache.at[slots].set(fresh)
    grouped = (queries.reshape(N_GROUP, GROUP_Q, D), positives.reshape(N_GROUP, GROUP_Q))
    grads, losses = lax.map(lambda pair: one_group(pair, updated), grouped)
    return (grads.reshape(QUERIES, D), losses.reshape(QUERIES))
```

```python
import functools
import math

import jax
import jax.numpy as jnp
from jax import lax
from jax.experimental import pallas as pl
from jax.experimental.pallas import tpu as pltpu
from jax.sharding import PartitionSpec as P

LANES = 128
LOG2E = math.log2(math.e)


def with_digits(rows, numbers, digits):
    parts = jnp.stack([(numbers >> (8 * k)) & 255 for k in range(digits)], axis=1)
    tail = jnp.pad(parts.astype(rows.dtype), ((0, 0), (0, LANES - digits)))
    return jnp.concatenate([rows, tail], axis=1)


def split3(x):
    hi = x.astype(jnp.bfloat16)
    rest = x - hi.astype(jnp.float32)
    mid = rest.astype(jnp.bfloat16)
    low = (rest - mid.astype(jnp.float32)).astype(jnp.bfloat16)
    return hi, mid, low


def partial_kernel(chunk, first_ref, got_ref, table_ref, out_ref, scores_ref):
    count, width = got_ref.shape
    depth = width - LANES
    rows = table_ref.shape[0]
    to_log2 = LOG2E / math.sqrt(depth)
    queries = got_ref[:, :depth]
    digits = got_ref[:, depth:].astype(jnp.float32)
    lane = lax.broadcasted_iota(jnp.int32, (1, LANES), 1)
    weight = jnp.where(lane == 0, 1.0, jnp.where(lane == 1, 256.0, jnp.where(lane == 2, 65536.0, 0.0)))
    where = jnp.sum(digits * weight, axis=1, keepdims=True) - first_ref[0].astype(jnp.float32)
    where = where.astype(jnp.int32)

    top = jnp.full((count, LANES), -jnp.inf, jnp.float32)
    for start in range(0, rows, chunk):
        part = lax.dot_general(
            queries, table_ref[start:start + chunk, :], (((1,), (1,)), ((), ())),
            preferred_element_type=jnp.float32,
        )
        scores_ref[:, start:start + chunk] = part
        for at in range(0, chunk, LANES):
            top = jnp.maximum(top, part[:, at:at + LANES])
    top = jnp.max(top, axis=1, keepdims=True) * to_log2

    total = jnp.zeros((count, LANES), jnp.float32)
    summed = jnp.zeros((count, depth), jnp.float32)
    picked = jnp.zeros((count, depth), jnp.float32)
    column = lax.broadcasted_iota(jnp.int32, (count, chunk), 1)
    for start in range(0, rows, chunk):
        weights = jnp.exp2(scores_ref[:, start:start + chunk] * to_log2 - top)
        for at in range(0, chunk, LANES):
            total = total + weights[:, at:at + LANES]
        block = table_ref[start:start + chunk, :]
        summed = summed + jnp.dot(weights.astype(jnp.bfloat16), block, preferred_element_type=jnp.float32)
        chosen = jnp.where(column == where - start, 1.0, 0.0).astype(jnp.bfloat16)
        picked = picked + jnp.dot(chosen, block, preferred_element_type=jnp.float32)
    total = jnp.sum(total, axis=1, keepdims=True)
    out_ref[:, :depth] = (summed / total).astype(jnp.bfloat16)
    out_ref[:, depth:2 * depth] = picked.astype(jnp.bfloat16)
    hi, mid, low = split3(jnp.broadcast_to(top + jnp.log2(total), (count, LANES)))
    zero = jnp.zeros((count, LANES), jnp.bfloat16)
    out_ref[:, 2 * depth:] = jnp.where(lane == 0, hi, jnp.where(lane == 1, mid, jnp.where(lane == 2, low, zero)))


def combine_kernel(got_ref, own_ref, grad_ref, loss_ref):
    sources, own, width = got_ref.shape
    depth = own_ref.shape[1]
    scale = 1.0 / math.sqrt(depth)
    tail = got_ref[:, :, 2 * depth:].astype(jnp.float32)
    logs = jnp.sum(tail, axis=2, keepdims=True)
    top = jnp.max(logs, axis=0, keepdims=True)
    share = jnp.exp2(logs - top)
    total = jnp.sum(share, axis=0)
    summed = jnp.sum(got_ref[:, :, :depth].astype(jnp.float32) * share, axis=0)
    positive = jnp.sum(got_ref[:, :, depth:2 * depth].astype(jnp.float32), axis=0)
    grad_ref[...] = (summed / total - positive) * scale
    pos_score = jnp.sum(own_ref[...].astype(jnp.float32) * positive, axis=1, keepdims=True) * scale
    loss = (top[0] + jnp.log2(total)) * (1.0 / LOG2E) - pos_score
    loss_ref[...] = jnp.broadcast_to(loss, (own, LANES))


def per_device(queries, positives, cache, fresh, slots):
    own, depth = queries.shape
    rows = cache.shape[0]
    shards = lax.axis_size("shard")
    groups = lax.axis_size("group")
    first = lax.axis_index("shard") * rows

    sent = with_digits(queries, positives, 3)
    got = lax.all_to_all(
        jnp.broadcast_to(sent[None], (shards,) + sent.shape), "shard", 0, 0
    ).reshape(shards * own, depth + LANES)

    new = with_digits(fresh, slots - first, 2)
    for bit in (1, 4, 2):
        other = lax.ppermute(new, "group", [(i, i ^ bit) for i in range(groups)])
        new = jnp.concatenate([new, other], axis=0)
    at = new[:, depth:depth + 2].astype(jnp.int32)
    table = cache.at[at[:, 0] + 256 * at[:, 1]].set(
        new[:, :depth], unique_indices=True, mode="promise_in_bounds"
    )

    vmem = pl.BlockSpec(memory_space=pltpu.VMEM)
    width = 2 * depth + LANES
    count = shards * own
    part = pl.pallas_call(
        functools.partial(partial_kernel, 512),
        out_shape=jax.ShapeDtypeStruct((count, width), jnp.bfloat16),
        in_specs=[pl.BlockSpec(memory_space=pltpu.SMEM), vmem, vmem],
        out_specs=vmem,
        scratch_shapes=[pltpu.VMEM((count, rows), jnp.float32)],
        compiler_params=pltpu.CompilerParams(vmem_limit_bytes=48 * 1024 * 1024),
        cost_estimate=pl.CostEstimate(
            flops=6 * count * rows * depth, bytes_accessed=2 * rows * depth, transcendentals=count * rows
        ),
    )(first.reshape(1).astype(jnp.int32), got, table)

    back = lax.all_to_all(part.reshape(shards, own, width), "shard", 0, 0)
    grad, loss = pl.pallas_call(
        combine_kernel,
        out_shape=(
            jax.ShapeDtypeStruct((own, depth), jnp.float32),
            jax.ShapeDtypeStruct((own, LANES), jnp.float32),
        ),
        in_specs=[vmem, vmem],
        out_specs=(vmem, vmem),
        compiler_params=pltpu.CompilerParams(vmem_limit_bytes=32 * 1024 * 1024),
    )(back, queries)
    return grad, loss[:, 0]


def solution(mesh):
    return jax.shard_map(
        per_device,
        mesh=mesh,
        in_specs=(
            P(("group", "shard"), None),
            P(("group", "shard")),
            P("shard", None),
            P(("group", "shard"), None),
            P(("group", "shard")),
        ),
        out_specs=(P(("group", "shard"), None), P(("group", "shard"))),
        check_vma=False,
    )
```

```python
import functools
import math

import jax
import jax.numpy as jnp
from jax import lax
from jax.experimental import pallas as pl
from jax.experimental.pallas import tpu as pltpu
from jax.sharding import PartitionSpec as P

LANES = 128
SLOTS = 4
PACKED = 64
LOG2E = math.log2(math.e)
NT = (((1,), (1,)), ((), ()))


def with_digits(rows, numbers, digits):
    parts = jnp.stack([(numbers >> (8 * k)) & 255 for k in range(digits)], axis=1)
    tail = jnp.pad(parts.astype(rows.dtype), ((0, 0), (0, LANES - digits)))
    return jnp.concatenate([rows, tail], axis=1)


def split3(x):
    hi = x.astype(jnp.bfloat16)
    rest = x - hi.astype(jnp.float32)
    mid = rest.astype(jnp.bfloat16)
    low = (rest - mid.astype(jnp.float32)).astype(jnp.bfloat16)
    return hi, mid, low


def iota(shape, dim):
    return lax.broadcasted_iota(jnp.int32, shape, dim)


def as_row(digit_rows, digits):
    turned = digit_rows.astype(jnp.float32).T
    row = turned[0:1]
    for k in range(1, digits):
        row = row + turned[k:k + 1] * 256.0**k
    return row


def plan_positives(pos, first, rows, own, shards):
    count = pos.shape[1]
    local = pos - first
    owned = (local >= 0.0) & (local < rows)
    holder = jnp.floor((pos + 0.5) * (1.0 / rows))
    lane = iota((1, count), 1)
    rank = jnp.zeros((1, count), jnp.float32)
    for k in range(1, own):
        same = (pltpu.roll(holder, k, 1) == holder) & (lane % own >= k)
        rank = rank + jnp.where(same, 1.0, 0.0)
    order = jnp.where(owned, 1.0, 0.0)
    k = 1
    while k < count:
        order = order + jnp.where(lane >= k, pltpu.roll(order, k, 1), 0.0)
        k *= 2
    hit = owned & (order == iota((PACKED, 1), 0).astype(jnp.float32) + 1.0)
    column = jnp.sum(jnp.where(hit, local + 1.0, 0.0), axis=1, keepdims=True) - 1.0
    place = ((lane // own) * SLOTS).astype(jnp.float32) + rank
    place = jnp.sum(jnp.where(hit, place + 1.0, 0.0), axis=1, keepdims=True) - 1.0
    held = jnp.sum(
        jnp.where(holder == iota((shards, 1), 0).astype(jnp.float32), 1.0, 0.0), axis=1, keepdims=True
    )
    spill = (jnp.max(rank) >= SLOTS) | (jnp.max(held) > PACKED)
    return column, place, spill


def partial_kernel(chunk, own, first_ref, got_ref, new_ref, table_ref, out_ref, spill_ref, scores_ref):
    count, width = got_ref.shape
    depth = width - LANES
    rows = table_ref.shape[0]
    extra = new_ref.shape[0]
    to_log2 = LOG2E / math.sqrt(depth)
    queries = got_ref[:, :depth]
    pos = as_row(got_ref[:, depth:], 3)
    column, place, spill = plan_positives(pos, first_ref[0].astype(jnp.float32), rows, own, count // own)
    spill_ref[0] = spill.astype(jnp.int32)

    new_digits = new_ref[:, depth:]
    new_row = as_row(new_digits, 2)
    weight = jnp.where(iota((1, LANES), 1) == 0, 1.0, jnp.where(iota((1, LANES), 1) == 1, 256.0, 0.0))
    new_column = jnp.sum(new_digits.astype(jnp.float32) * weight, axis=1, keepdims=True)

    spans = [(start, chunk) for start in range(0, rows, chunk)] + [(rows, extra)]

    def block_of(start, size):
        return new_ref[:, :depth] if start == rows else table_ref[start:start + size, :]

    names = []
    top = jnp.full((count, LANES), -jnp.inf, jnp.float32)
    for start, size in spans:
        part = lax.dot_general(queries, block_of(start, size), NT, preferred_element_type=jnp.float32)
        if start == rows:
            name = new_row
        else:
            name = (iota((1, size), 1) + start).astype(jnp.float32)
            gone = jnp.max(jnp.where(new_column == name, 1.0, 0.0), axis=0, keepdims=True) > 0.0
            name = jnp.where(gone, -2.0, name)
            part = jnp.where(gone, -jnp.inf, part)
        names.append(name)
        scores_ref[:, start:start + size] = part
        for at in range(0, size, LANES):
            top = jnp.maximum(top, part[:, at:at + LANES])
    top = jnp.max(top, axis=1, keepdims=True) * to_log2

    total = jnp.zeros((count, LANES), jnp.float32)
    summed = jnp.zeros((count + PACKED, depth), jnp.float32)
    for (start, size), name in zip(spans, names):
        weights = jnp.exp2(scores_ref[:, start:start + size] * to_log2 - top)
        for at in range(0, size, LANES):
            total = total + weights[:, at:at + LANES]
        chosen = jnp.where(column == name, 1.0, 0.0)
        both = jnp.concatenate([weights.astype(jnp.bfloat16), chosen.astype(jnp.bfloat16)], axis=0)
        summed = summed + jnp.dot(both, block_of(start, size), preferred_element_type=jnp.float32)
    total = jnp.sum(total, axis=1, keepdims=True)
    out_ref[:, :depth] = (summed[:count] / total).astype(jnp.bfloat16)

    packed = summed[count:].astype(jnp.bfloat16)
    place_row = jnp.broadcast_to(place, (PACKED, LANES)).T[0:1]
    row = iota((count, 1), 0)
    slot = (row // own) * SLOTS + (row % own) // 2
    spread = jnp.where(slot.astype(jnp.float32) == place_row, 1.0, 0.0).astype(jnp.bfloat16)
    spread = jnp.dot(spread, packed, preferred_element_type=jnp.float32)
    half = depth // 2
    out_ref[:, depth:depth + half] = jnp.where(row % 2 == 0, spread[:, :half], spread[:, half:]).astype(jnp.bfloat16)

    hi, mid, low = split3(jnp.broadcast_to(top + jnp.log2(total), (count, LANES)))
    lane = iota((1, LANES), 1)
    zero = jnp.zeros((count, LANES), jnp.bfloat16)
    out_ref[:, depth + half:] = jnp.where(lane == 0, hi, jnp.where(lane == 1, mid, jnp.where(lane == 2, low, zero)))


def combine(got_ref, own_ref, positive, grad_ref, loss_ref):
    own, depth = own_ref.shape
    scale = 1.0 / math.sqrt(depth)
    logs = jnp.sum(got_ref[:, :, depth + depth // 2:].astype(jnp.float32), axis=2, keepdims=True)
    top = jnp.max(logs, axis=0, keepdims=True)
    share = jnp.exp2(logs - top)
    total = jnp.sum(share, axis=0)
    summed = jnp.sum(got_ref[:, :, :depth].astype(jnp.float32) * share, axis=0)
    grad_ref[...] = (summed / total - positive) * scale
    pos_score = jnp.sum(own_ref[...].astype(jnp.float32) * positive, axis=1, keepdims=True) * scale
    loss = (top[0] + jnp.log2(total)) * (1.0 / LOG2E) - pos_score
    loss_ref[...] = jnp.broadcast_to(loss, (own, LANES))


def slots_kernel(rows, pos_ref, got_ref, own_ref, grad_ref, loss_ref):
    own, depth = own_ref.shape
    half = depth // 2
    holders = [pos_ref[a] // rows for a in range(own)]
    positive = jnp.zeros((own, depth), jnp.float32)
    line = iota((own, 1), 0)
    for a in range(own):
        slot = 0
        for b in range(a):
            slot = slot + jnp.where(holders[b] == holders[a], 1, 0)
        block = got_ref[holders[a], :, depth:depth + half].astype(jnp.float32)
        left = jnp.sum(jnp.where(line == 2 * slot, block, 0.0), axis=0, keepdims=True)
        right = jnp.sum(jnp.where(line == 2 * slot + 1, block, 0.0), axis=0, keepdims=True)
        positive = jnp.where(line == a, jnp.concatenate([left, right], axis=1), positive)
    combine(got_ref, own_ref, positive, grad_ref, loss_ref)


def rows_kernel(got_ref, own_ref, positive_ref, grad_ref, loss_ref):
    combine(got_ref, own_ref, positive_ref[...], grad_ref, loss_ref)


def per_device(queries, positives, cache, fresh, slots):
    own, depth = queries.shape
    rows = cache.shape[0]
    shards = lax.axis_size("shard")
    groups = lax.axis_size("group")
    count = shards * own
    first = lax.axis_index("shard") * rows

    sent = with_digits(queries, positives, 3)
    got = lax.all_to_all(
        jnp.broadcast_to(sent[None], (shards,) + sent.shape), "shard", 0, 0
    ).reshape(count, depth + LANES)

    new = with_digits(fresh, slots - first, 2)
    for bit in (1, 4, 2):
        other = lax.ppermute(new, "group", [(i, i ^ bit) for i in range(groups)])
        new = jnp.concatenate([new, other], axis=0)

    vmem = pl.BlockSpec(memory_space=pltpu.VMEM)
    smem = pl.BlockSpec(memory_space=pltpu.SMEM)
    width = depth + depth // 2 + LANES
    part, spill = pl.pallas_call(
        functools.partial(partial_kernel, 512, own),
        out_shape=(
            jax.ShapeDtypeStruct((count, width), jnp.bfloat16),
            jax.ShapeDtypeStruct((1,), jnp.int32),
        ),
        in_specs=[smem, vmem, vmem, vmem],
        out_specs=(vmem, smem),
        scratch_shapes=[pltpu.VMEM((count, rows + new.shape[0]), jnp.float32)],
        compiler_params=pltpu.CompilerParams(vmem_limit_bytes=48 * 1024 * 1024),
        cost_estimate=pl.CostEstimate(
            flops=4 * count * rows * depth, bytes_accessed=2 * rows * depth, transcendentals=count * rows
        ),
    )(first.reshape(1).astype(jnp.int32), got, new, cache)

    back = lax.all_to_all(part.reshape(shards, own, width), "shard", 0, 0)
    outs = (
        jax.ShapeDtypeStruct((own, depth), jnp.float32),
        jax.ShapeDtypeStruct((own, LANES), jnp.float32),
    )
    params = pltpu.CompilerParams(vmem_limit_bytes=32 * 1024 * 1024)

    def from_slots():
        return pl.pallas_call(
            functools.partial(slots_kernel, rows), out_shape=outs,
            in_specs=[smem, vmem, vmem], out_specs=(vmem, vmem), compiler_params=params,
        )(positives, back, queries)

    def from_rows():
        digits = got[:, depth:depth + 3].astype(jnp.int32)
        local = digits[:, 0] + 256 * digits[:, 1] + 65536 * digits[:, 2] - first
        at = new[:, depth:depth + 2].astype(jnp.int32)
        is_new = local[:, None] == (at[:, 0] + 256 * at[:, 1])[None, :]
        new_rows = jnp.dot(
            is_new.astype(jnp.bfloat16), new[:, :depth], preferred_element_type=jnp.float32
        ).astype(jnp.bfloat16)
        old_rows = cache[jnp.clip(local, 0, rows - 1)]
        owned = (local >= 0) & (local < rows)
        picked = jnp.where(jnp.any(is_new, axis=1)[:, None], new_rows, jnp.where(owned[:, None], old_rows, 0))
        picked = lax.all_to_all(picked.reshape(shards, own, depth), "shard", 0, 0)
        positive = jnp.sum(picked.astype(jnp.float32), axis=0)
        return pl.pallas_call(
            rows_kernel, out_shape=outs,
            in_specs=[vmem, vmem, vmem], out_specs=(vmem, vmem), compiler_params=params,
        )(back, queries, positive)

    grad, loss = lax.cond(spill[0] > 0, from_rows, from_slots)
    return grad, loss[:, 0]


def solution(mesh):
    return jax.shard_map(
        per_device,
        mesh=mesh,
        in_specs=(
            P(("group", "shard"), None),
            P(("group", "shard")),
            P("shard", None),
            P(("group", "shard"), None),
            P(("group", "shard")),
        ),
        out_specs=(P(("group", "shard"), None), P(("group", "shard"))),
        check_vma=False,
    )
```

```python
import functools
import math

import jax
import jax.numpy as jnp
from jax import lax
from jax.experimental import pallas as pl
from jax.experimental.pallas import tpu as pltpu
from jax.sharding import PartitionSpec as P

LANES = 128
SIDE = 8
SLOTS = 12
TAIL = 16
CHUNK = 1024
PACKED = 64
LOG2E = math.log2(math.e)
NT = (((1,), (1,)), ((), ()))


def with_digits(rows, numbers, digits):
    parts = jnp.stack([(numbers >> (8 * k)) & 255 for k in range(digits)], axis=1)
    tail = jnp.pad(parts.astype(rows.dtype), ((0, 0), (0, LANES - digits)))
    return jnp.concatenate([rows, tail], axis=1)


def sent_kernel(digits, pos_ref, rows_ref, out_ref):
    own, depth = rows_ref.shape
    line, lane = iota((own, LANES), 0), iota((own, LANES), 1)
    tail = jnp.zeros((own, LANES), jnp.float32)
    for a in range(own):
        for k in range(digits):
            digit = ((pos_ref[a] >> (8 * k)) & 255).astype(jnp.float32)
            tail = jnp.where((line == a) & (lane == k), digit, tail)
    whole = jnp.concatenate([rows_ref[...], tail.astype(rows_ref.dtype)], axis=1)
    out_ref[...] = jnp.broadcast_to(whole[None], out_ref.shape)


def split3(x):
    hi = x.astype(jnp.bfloat16)
    rest = x - hi.astype(jnp.float32)
    mid = rest.astype(jnp.bfloat16)
    low = (rest - mid.astype(jnp.float32)).astype(jnp.bfloat16)
    return hi, mid, low


def iota(shape, dim):
    return lax.broadcasted_iota(jnp.int32, shape, dim)


def as_row(digit_rows, digits):
    turned = digit_rows.astype(jnp.float32).T
    row = turned[0:1]
    for k in range(1, digits):
        row = row + turned[k:k + 1] * 256.0**k
    return row


def plan_positives(pos, first, rows, shards, sides):
    count = pos.shape[1]
    local = pos - first
    owned = (local >= 0.0) & (local < rows)
    holder = jnp.floor((pos + 0.5) * (1.0 / rows))
    lane = iota((1, count), 1)
    block = lane // (count // sides)
    order = jnp.where(owned, 1.0, 0.0)
    k = 1
    while k < count:
        order = order + jnp.where(lane >= k, pltpu.roll(order, k, 1), 0.0)
        k *= 2
    before = jnp.zeros((1, count), jnp.float32)
    held = jnp.zeros((shards, 1), jnp.float32)
    most = 0.0
    is_holder = jnp.where(holder == iota((shards, 1), 0).astype(jnp.float32), 1.0, 0.0)
    for b in range(sides):
        here = block == b
        earlier = jnp.max(jnp.where(block < b, order, 0.0))
        before = jnp.where(here, earlier, before)
        part = jnp.sum(jnp.where(here, is_holder, 0.0), axis=1, keepdims=True)
        most = jnp.maximum(most, jnp.max(part))
        held = held + part
    spill = (most > SLOTS) | (jnp.max(held) > PACKED)
    slot = jnp.where(owned, order - before, 0.0)
    place = jnp.where(slot <= SLOTS, (block * TAIL).astype(jnp.float32) + slot, 0.0)
    hit = owned & (order == iota((PACKED, 1), 0).astype(jnp.float32) + 1.0)
    column = jnp.sum(jnp.where(hit, local + 1.0, 0.0), axis=1, keepdims=True) - 1.0
    place = jnp.sum(jnp.where(hit, place, 0.0), axis=1, keepdims=True) - 1.0
    return column, place, slot, spill


def partial_kernel(chunk, shards, first_ref, got_ref, new_ref, cache_ref, out_ref, spill_ref, table_ref, scores_ref, both_ref, sems):
    count, width = got_ref.shape
    depth = width - LANES
    rows = cache_ref.shape[0]
    extra = new_ref.shape[0]
    to_log2 = LOG2E / math.sqrt(depth)
    loads = []
    for start in range(0, rows, chunk):
        span = pl.ds(start, chunk)
        loads.append(pltpu.make_async_copy(cache_ref.at[span, :], table_ref.at[span, :], sems.at[start // chunk]))
        if len(loads) <= 2:
            loads[-1].start()
    pos = as_row(got_ref[:, depth:], 3)
    column, place, slot, spill = plan_positives(pos, first_ref[0].astype(jnp.float32), rows, shards, SIDE)
    spill_ref[0] = spill.astype(jnp.int32)

    new_digits = new_ref[:, depth:]
    new_row = as_row(new_digits, 2)
    weight = jnp.where(iota((1, LANES), 1) == 0, 1.0, jnp.where(iota((1, LANES), 1) == 1, 256.0, 0.0))
    new_column = jnp.sum(new_digits.astype(jnp.float32) * weight, axis=1, keepdims=True)

    spans = [(start, chunk) for start in range(0, rows, chunk)] + [(rows, extra)]

    def block_of(start, size):
        return new_ref[:, :depth] if start == rows else table_ref[start:start + size, :]

    names, dead = [], []
    for start, size in spans:
        name, gone = new_row, None
        if start < rows:
            name = (iota((1, size), 1) + start).astype(jnp.float32)
            gone = jnp.max(jnp.where(new_column == name, 1.0, 0.0), axis=0, keepdims=True) > 0.0
            name = jnp.where(gone, -2.0, name)
        names.append(name)
        dead.append(gone)
    for (start, size), name in zip(spans, names):
        both_ref[count:, start:start + size] = jnp.where(column == name, 1.0, 0.0).astype(jnp.bfloat16)

    part_count = count // 2
    tops, totals = [], []
    for at_row in (0, part_count):
        mine = slice(at_row, at_row + part_count)
        top = jnp.full((part_count, LANES), -jnp.inf, jnp.float32)
        for (start, size), gone in zip(spans, dead):
            if at_row == 0 and start < rows:
                loads[start // chunk].wait()
                if start // chunk + 2 < len(loads):
                    loads[start // chunk + 2].start()
            part = lax.dot_general(
                got_ref[mine, :depth], block_of(start, size), NT, preferred_element_type=jnp.float32
            )
            if gone is not None:
                part = jnp.where(gone, -jnp.inf, part)
            scores_ref[mine, start:start + size] = part
            for at in range(0, size, LANES):
                top = jnp.maximum(top, part[:, at:at + LANES])
        top = jnp.max(top, axis=1, keepdims=True) * to_log2
        total = jnp.zeros((part_count, LANES), jnp.float32)
        for start, size in spans:
            weights = jnp.exp2(scores_ref[mine, start:start + size] * to_log2 - top)
            for at in range(0, size, LANES):
                total = total + weights[:, at:at + LANES]
            both_ref[mine, start:start + size] = weights.astype(jnp.bfloat16)
        tops.append(top)
        totals.append(total)
    top, total = jnp.concatenate(tops, axis=0), jnp.concatenate(totals, axis=0)
    sums = []
    for mine in (slice(0, part_count), slice(part_count, count + PACKED)):
        part = jnp.dot(both_ref[mine, :rows], table_ref[...], preferred_element_type=jnp.float32)
        sums.append(part + jnp.dot(both_ref[mine, rows:], new_ref[:, :depth], preferred_element_type=jnp.float32))
    summed = jnp.concatenate(sums, axis=0)
    total = jnp.sum(total, axis=1, keepdims=True)
    mean = (summed[:count] / total).astype(jnp.bfloat16)

    packed = summed[count:].astype(jnp.bfloat16)
    place_row = jnp.broadcast_to(place, (PACKED, LANES)).T[0:1]
    spread = jnp.where(iota((SIDE * TAIL, 1), 0).astype(jnp.float32) == place_row, 1.0, 0.0).astype(jnp.bfloat16)
    spread = jnp.dot(spread, packed, preferred_element_type=jnp.float32)
    logs = jnp.broadcast_to(top + jnp.log2(total), (count, LANES)).T[0:1]
    facts = [part.astype(jnp.float32) for part in split3(logs)] + [slot]
    block = count // SIDE
    line, lane = iota((TAIL, LANES), 0), iota((TAIL, LANES), 1)
    for b in range(SIDE):
        at = b * block // LANES * LANES
        tail = spread[b * TAIL:(b + 1) * TAIL]
        first_tile = tail[:, :LANES]
        for k, fact in enumerate(facts):
            piece = fact[:, at:at + LANES]
            if b * block % LANES:
                piece = pltpu.roll(piece, LANES - b * block % LANES, 1)
            first_tile = jnp.where((line == SLOTS + k) & (lane < block), piece, first_tile)
        out_ref[b, :block, :] = mean[b * block:(b + 1) * block]
        out_ref[b, block:, :LANES] = first_tile.astype(jnp.bfloat16)
        out_ref[b, block:, LANES:] = tail[:, LANES:].astype(jnp.bfloat16)


def block_kernel(got_ref, out_ref):
    sources, lines, depth = got_ref.shape
    block = lines - TAIL
    source = iota((sources, LANES), 0)
    logs = jnp.zeros((sources, LANES), jnp.float32)
    slot = jnp.zeros((sources, LANES), jnp.float32)
    for s in range(sources):
        tail = got_ref[s, block:, :LANES].astype(jnp.float32)
        log = tail[SLOTS:SLOTS + 1] + tail[SLOTS + 1:SLOTS + 2] + tail[SLOTS + 2:SLOTS + 3]
        logs = jnp.where(source == s, log, logs)
        slot = jnp.where(source == s, tail[SLOTS + 3:SLOTS + 4], slot)
    top = jnp.max(logs, axis=0, keepdims=True)
    share = jnp.exp2(logs - top)
    total = jnp.sum(share, axis=0, keepdims=True)
    share = share / total
    whole = jnp.broadcast_to(top + jnp.log2(total), (sources, LANES))
    rest = jnp.zeros((LANES - 3 * sources, LANES), jnp.float32)
    turned = jnp.concatenate([share, slot, whole, rest], axis=0).T[:block]

    summed = jnp.zeros((block, depth), jnp.float32)
    for s in range(sources):
        summed = summed + got_ref[s, :block, :].astype(jnp.float32) * turned[:, s:s + 1]
    lane = iota((1, sources * TAIL), 1)
    wanted = jnp.zeros((block, sources * TAIL), jnp.float32)
    for s in range(sources):
        wanted = jnp.where(lane // TAIL == s, turned[:, sources + s:sources + s + 1], wanted)
    chosen = jnp.where(wanted == (lane % TAIL + 1).astype(jnp.float32), 1.0, 0.0).astype(jnp.bfloat16)
    slots = jnp.concatenate([got_ref[s, block:, :] for s in range(sources)], axis=0)
    positive = jnp.dot(chosen, slots, preferred_element_type=jnp.float32)
    out_ref[:, :depth] = summed.astype(jnp.bfloat16)
    out_ref[:, depth:2 * depth] = positive.astype(jnp.bfloat16)
    hi, mid, low = split3(jnp.broadcast_to(turned[:, 2 * sources:2 * sources + 1], (block, LANES)))
    lane = iota((1, LANES), 1)
    zero = jnp.zeros((block, LANES), jnp.bfloat16)
    out_ref[:, 2 * depth:] = jnp.where(lane == 0, hi, jnp.where(lane == 1, mid, jnp.where(lane == 2, low, zero)))


def combine(got_ref, own_ref, positive, grad_ref, loss_ref):
    own, depth = own_ref.shape
    scale = 1.0 / math.sqrt(depth)
    logs = jnp.sum(got_ref[:, :, 2 * depth:].astype(jnp.float32), axis=2, keepdims=True)
    top = jnp.max(logs, axis=0, keepdims=True)
    share = jnp.exp2(logs - top)
    total = jnp.sum(share, axis=0)
    summed = jnp.sum(got_ref[:, :, :depth].astype(jnp.float32) * share, axis=0)
    grad_ref[...] = (summed / total - positive) * scale
    pos_score = jnp.sum(own_ref[...].astype(jnp.float32) * positive, axis=1, keepdims=True) * scale
    loss = (top[0] + jnp.log2(total)) * (1.0 / LOG2E) - pos_score
    line, lane = iota((own, LANES), 0), iota((own, LANES), 1)
    loss_ref[...] = jnp.sum(jnp.where(line == lane, loss, 0.0), axis=0, keepdims=True)


def slots_kernel(got_ref, own_ref, grad_ref, loss_ref):
    depth = own_ref.shape[1]
    positive = jnp.sum(got_ref[:, :, depth:2 * depth].astype(jnp.float32), axis=0)
    combine(got_ref, own_ref, positive, grad_ref, loss_ref)


def rows_kernel(got_ref, own_ref, positive_ref, grad_ref, loss_ref):
    combine(got_ref, own_ref, positive_ref[...], grad_ref, loss_ref)


def routes(groups):
    plane, first_ring, second_ring = [], [], []
    for g in range(groups):
        table = [[g * SIDE * SIDE + z * SIDE + y for y in range(SIDE)] for z in range(SIDE)]
        turned = [list(column) for column in zip(*table)]
        if g % 2:
            table, turned = turned, table
        plane.append([device for row in table for device in row])
        first_ring += turned
        second_ring += table
    return plane, first_ring, second_ring


def per_device(queries, positives, cache, fresh, slots):
    own, depth = queries.shape
    rows = cache.shape[0]
    shards = lax.axis_size("shard")
    groups = lax.axis_size("group")
    count = shards * own
    every = ("group", "shard")
    plane, first_ring, second_ring = routes(groups)
    first = lax.axis_index("shard") * rows

    vmem = pl.BlockSpec(memory_space=pltpu.VMEM)
    smem = pl.BlockSpec(memory_space=pltpu.SMEM)
    sent = pl.pallas_call(
        functools.partial(sent_kernel, 3),
        out_shape=pltpu.VMEM((shards, own, depth + LANES), jnp.bfloat16),
        in_specs=[smem, vmem], out_specs=vmem,
    )(positives, queries)
    got = lax.all_to_all(sent, every, 0, 0, axis_index_groups=plane).reshape(count, depth + LANES)

    new = with_digits(fresh, slots - first, 2)
    for bit in (1, 4, 2):
        other = lax.ppermute(new, "group", [(i, i ^ bit) for i in range(groups)])
        new = jnp.concatenate([new, other], axis=0)

    block = count // SIDE
    width = 2 * depth + LANES
    part, spill = pl.pallas_call(
        functools.partial(partial_kernel, CHUNK, shards),
        out_shape=(
            pltpu.VMEM((SIDE, block + TAIL, depth), jnp.bfloat16),
            jax.ShapeDtypeStruct((1,), jnp.int32),
        ),
        in_specs=[smem, vmem, vmem, pl.BlockSpec(memory_space=pl.ANY)],
        out_specs=(vmem, smem),
        scratch_shapes=[
            pltpu.VMEM((rows, depth), jnp.bfloat16),
            pltpu.VMEM((count, rows + new.shape[0]), jnp.float32),
            pltpu.VMEM((count + PACKED, rows + new.shape[0]), jnp.bfloat16),
            pltpu.SemaphoreType.DMA((rows // CHUNK,)),
        ],
        compiler_params=pltpu.CompilerParams(vmem_limit_bytes=48 * 1024 * 1024),
        cost_estimate=pl.CostEstimate(
            flops=4 * count * rows * depth, bytes_accessed=2 * rows * depth, transcendentals=count * rows
        ),
    )(first.reshape(1).astype(jnp.int32), got, new, cache)

    part = lax.all_to_all(part, every, 0, 0, axis_index_groups=first_ring)
    part = pl.pallas_call(
        block_kernel,
        out_shape=pltpu.VMEM((block, width), jnp.bfloat16),
        in_specs=[vmem], out_specs=vmem,
        compiler_params=pltpu.CompilerParams(vmem_limit_bytes=32 * 1024 * 1024),
    )(part)
    back = lax.all_to_all(part.reshape(SIDE, own, width), every, 0, 0, axis_index_groups=second_ring)
    outs = (
        jax.ShapeDtypeStruct((own, depth), jnp.float32),
        jax.ShapeDtypeStruct((1, LANES), jnp.float32),
    )
    params = pltpu.CompilerParams(vmem_limit_bytes=32 * 1024 * 1024)

    def from_slots():
        return pl.pallas_call(
            slots_kernel, out_shape=outs,
            in_specs=[vmem, vmem], out_specs=(vmem, vmem), compiler_params=params,
        )(back, queries)

    def from_rows():
        digits = got[:, depth:depth + 3].astype(jnp.int32)
        local = digits[:, 0] + 256 * digits[:, 1] + 65536 * digits[:, 2] - first
        at = new[:, depth:depth + 2].astype(jnp.int32)
        is_new = local[:, None] == (at[:, 0] + 256 * at[:, 1])[None, :]
        new_rows = jnp.dot(
            is_new.astype(jnp.bfloat16), new[:, :depth], preferred_element_type=jnp.float32
        ).astype(jnp.bfloat16)
        old_rows = cache[jnp.clip(local, 0, rows - 1)]
        owned = (local >= 0) & (local < rows)
        picked = jnp.where(jnp.any(is_new, axis=1)[:, None], new_rows, jnp.where(owned[:, None], old_rows, 0))
        picked = lax.all_to_all(picked.reshape(shards, own, depth), every, 0, 0, axis_index_groups=plane)
        positive = jnp.sum(picked.astype(jnp.float32), axis=0)
        return pl.pallas_call(
            rows_kernel, out_shape=outs,
            in_specs=[vmem, vmem, vmem], out_specs=(vmem, vmem), compiler_params=params,
        )(back, queries, positive)

    grad, loss = lax.cond(spill[0] > 0, from_rows, from_slots)
    return grad, loss[0, :own]


def solution(mesh):
    return jax.shard_map(
        per_device,
        mesh=mesh,
        in_specs=(
            P(("group", "shard"), None),
            P(("group", "shard")),
            P("shard", None),
            P(("group", "shard"), None),
            P(("group", "shard")),
        ),
        out_specs=(P(("group", "shard"), None), P(("group", "shard"))),
        check_vma=False,
    )
```

```python
import functools
import math

import jax
import jax.numpy as jnp
from jax import lax
from jax.experimental import pallas as pl
from jax.experimental.pallas import tpu as pltpu
from jax.sharding import PartitionSpec as P

LANES = 128
SIDE = 8
SLOTS = 12
TAIL = 16
CHUNK = 1024
PACKED = 64
LOG2E = math.log2(math.e)
NT = (((1,), (1,)), ((), ()))


def with_digits(numbers, rows, digits):
    line, lane = iota((len(numbers), LANES), 0), iota((len(numbers), LANES), 1)
    tail = jnp.zeros((len(numbers), LANES), jnp.float32)
    for n, number in enumerate(numbers):
        for k in range(digits):
            digit = ((number >> (8 * k)) & 255).astype(jnp.float32)
            tail = jnp.where((line == n) & (lane == k), digit, tail)
    return jnp.concatenate([rows, tail.astype(rows.dtype)], axis=1)


def sent_kernel(first_ref, pos_ref, slots_ref, queries_ref, fresh_ref, out_ref, new_ref):
    own, added = queries_ref.shape[0], fresh_ref.shape[0]
    whole = with_digits([pos_ref[n] for n in range(own)], queries_ref[...], 3)
    out_ref[...] = jnp.broadcast_to(whole[None], out_ref.shape)
    new_ref[...] = with_digits([slots_ref[n] - first_ref[0] for n in range(added)], fresh_ref[...], 2)


def split3(x):
    hi = x.astype(jnp.bfloat16)
    rest = x - hi.astype(jnp.float32)
    mid = rest.astype(jnp.bfloat16)
    low = (rest - mid.astype(jnp.float32)).astype(jnp.bfloat16)
    return hi, mid, low


def iota(shape, dim):
    return lax.broadcasted_iota(jnp.int32, shape, dim)


def as_row(digit_rows, digits):
    turned = digit_rows.astype(jnp.float32).T
    row = turned[0:1]
    for k in range(1, digits):
        row = row + turned[k:k + 1] * 256.0**k
    return row


def plan_positives(pos, first, rows, shards, sides):
    count = pos.shape[1]
    local = pos - first
    owned = (local >= 0.0) & (local < rows)
    holder = jnp.floor((pos + 0.5) * (1.0 / rows))
    lane = iota((1, count), 1)
    block = lane // (count // sides)
    order = jnp.where(owned, 1.0, 0.0)
    k = 1
    while k < count:
        order = order + jnp.where(lane >= k, pltpu.roll(order, k, 1), 0.0)
        k *= 2
    before = jnp.zeros((1, count), jnp.float32)
    held = jnp.zeros((shards, 1), jnp.float32)
    most = 0.0
    is_holder = jnp.where(holder == iota((shards, 1), 0).astype(jnp.float32), 1.0, 0.0)
    for b in range(sides):
        here = block == b
        earlier = jnp.max(jnp.where(block < b, order, 0.0))
        before = jnp.where(here, earlier, before)
        part = jnp.sum(jnp.where(here, is_holder, 0.0), axis=1, keepdims=True)
        most = jnp.maximum(most, jnp.max(part))
        held = held + part
    spill = (most > SLOTS) | (jnp.max(held) > PACKED)
    slot = jnp.where(owned, order - before, 0.0)
    place = jnp.where(slot <= SLOTS, (block * TAIL).astype(jnp.float32) + slot, 0.0)
    hit = owned & (order == iota((PACKED, 1), 0).astype(jnp.float32) + 1.0)
    column = jnp.sum(jnp.where(hit, local + 1.0, 0.0), axis=1, keepdims=True) - 1.0
    place = jnp.sum(jnp.where(hit, place, 0.0), axis=1, keepdims=True) - 1.0
    return column, place, slot, spill


def partial_kernel(chunk, shards, first_ref, got_ref, *refs):
    *new_refs, cache_ref, out_ref, spill_ref, table_ref, new_ref, scores_ref, both_ref, sem = refs
    count, width = got_ref.shape
    depth = width - LANES
    rows = cache_ref.shape[0]
    extra = new_ref.shape[0]
    to_log2 = LOG2E / math.sqrt(depth)
    load = pltpu.make_async_copy(cache_ref, table_ref, sem)
    load.start()
    piece = extra // len(new_refs)
    for n, ref in enumerate(new_refs):
        new_ref[n * piece:(n + 1) * piece, :] = ref[...]
    pos = as_row(got_ref[:, depth:], 3)
    column, place, slot, spill = plan_positives(pos, first_ref[0].astype(jnp.float32), rows, shards, SIDE)
    spill_ref[0] = spill.astype(jnp.int32)

    new_digits = new_ref[:, depth:]
    new_row = as_row(new_digits, 2)
    weight = jnp.where(iota((1, LANES), 1) == 0, 1.0, jnp.where(iota((1, LANES), 1) == 1, 256.0, 0.0))
    new_column = jnp.sum(new_digits.astype(jnp.float32) * weight, axis=1, keepdims=True)

    spans = [(start, chunk) for start in range(0, rows, chunk)] + [(rows, extra)]

    def block_of(start, size):
        return new_ref[:, :depth] if start == rows else table_ref[start:start + size, :]

    names, dead = [], []
    for start, size in spans:
        name, gone = new_row, None
        if start < rows:
            name = (iota((1, size), 1) + start).astype(jnp.float32)
            gone = jnp.max(jnp.where(new_column == name, 1.0, 0.0), axis=0, keepdims=True) > 0.0
            name = jnp.where(gone, -2.0, name)
        names.append(name)
        dead.append(gone)
    for (start, size), name in zip(spans, names):
        both_ref[count:, start:start + size] = jnp.where(column == name, 1.0, 0.0).astype(jnp.bfloat16)

    load.wait()
    part_count = count // 2
    tops, totals = [], []
    for at_row in (0, part_count):
        mine = slice(at_row, at_row + part_count)
        top = jnp.full((part_count, LANES), -jnp.inf, jnp.float32)
        for (start, size), gone in zip(spans, dead):
            part = lax.dot_general(
                got_ref[mine, :depth], block_of(start, size), NT, preferred_element_type=jnp.float32
            )
            if gone is not None:
                part = jnp.where(gone, -jnp.inf, part)
            scores_ref[mine, start:start + size] = part
            for at in range(0, size, LANES):
                top = jnp.maximum(top, part[:, at:at + LANES])
        top = jnp.max(top, axis=1, keepdims=True) * to_log2
        total = jnp.zeros((part_count, LANES), jnp.float32)
        for start, size in spans:
            weights = jnp.exp2(scores_ref[mine, start:start + size] * to_log2 - top)
            for at in range(0, size, LANES):
                total = total + weights[:, at:at + LANES]
            both_ref[mine, start:start + size] = weights.astype(jnp.bfloat16)
        tops.append(top)
        totals.append(total)
    top, total = jnp.concatenate(tops, axis=0), jnp.concatenate(totals, axis=0)
    sums = []
    for mine in (slice(0, part_count), slice(part_count, count + PACKED)):
        part = jnp.dot(both_ref[mine, :rows], table_ref[...], preferred_element_type=jnp.float32)
        sums.append(part + jnp.dot(both_ref[mine, rows:], new_ref[:, :depth], preferred_element_type=jnp.float32))
    summed = jnp.concatenate(sums, axis=0)
    total = jnp.sum(total, axis=1, keepdims=True)
    mean = (summed[:count] / total).astype(jnp.bfloat16)

    packed = summed[count:].astype(jnp.bfloat16)
    place_row = jnp.broadcast_to(place, (PACKED, LANES)).T[0:1]
    spread = jnp.where(iota((SIDE * TAIL, 1), 0).astype(jnp.float32) == place_row, 1.0, 0.0).astype(jnp.bfloat16)
    spread = jnp.dot(spread, packed, preferred_element_type=jnp.float32)
    logs = jnp.broadcast_to(top + jnp.log2(total), (count, LANES)).T[0:1]
    facts = [part.astype(jnp.float32) for part in split3(logs)] + [slot]
    block = count // SIDE
    line, lane = iota((TAIL, LANES), 0), iota((TAIL, LANES), 1)
    for b in range(SIDE):
        at = b * block // LANES * LANES
        tail = spread[b * TAIL:(b + 1) * TAIL]
        first_tile = tail[:, :LANES]
        for k, fact in enumerate(facts):
            piece = fact[:, at:at + LANES]
            if b * block % LANES:
                piece = pltpu.roll(piece, LANES - b * block % LANES, 1)
            first_tile = jnp.where((line == SLOTS + k) & (lane < block), piece, first_tile)
        out_ref[b, :block, :] = mean[b * block:(b + 1) * block]
        out_ref[b, block:, :LANES] = first_tile.astype(jnp.bfloat16)
        out_ref[b, block:, LANES:] = tail[:, LANES:].astype(jnp.bfloat16)


def block_kernel(got_ref, out_ref):
    sources, lines, depth = got_ref.shape
    block = lines - TAIL
    source = iota((sources, LANES), 0)
    logs = jnp.zeros((sources, LANES), jnp.float32)
    slot = jnp.zeros((sources, LANES), jnp.float32)
    for s in range(sources):
        tail = got_ref[s, block:, :LANES].astype(jnp.float32)
        log = tail[SLOTS:SLOTS + 1] + tail[SLOTS + 1:SLOTS + 2] + tail[SLOTS + 2:SLOTS + 3]
        logs = jnp.where(source == s, log, logs)
        slot = jnp.where(source == s, tail[SLOTS + 3:SLOTS + 4], slot)
    top = jnp.max(logs, axis=0, keepdims=True)
    share = jnp.exp2(logs - top)
    total = jnp.sum(share, axis=0, keepdims=True)
    share = share / total
    whole = jnp.broadcast_to(top + jnp.log2(total), (sources, LANES))
    rest = jnp.zeros((LANES - 3 * sources, LANES), jnp.float32)
    turned = jnp.concatenate([share, slot, whole, rest], axis=0).T[:block]

    summed = jnp.zeros((block, depth), jnp.float32)
    for s in range(sources):
        summed = summed + got_ref[s, :block, :].astype(jnp.float32) * turned[:, s:s + 1]
    lane = iota((1, sources * TAIL), 1)
    wanted = jnp.zeros((block, sources * TAIL), jnp.float32)
    for s in range(sources):
        wanted = jnp.where(lane // TAIL == s, turned[:, sources + s:sources + s + 1], wanted)
    chosen = jnp.where(wanted == (lane % TAIL + 1).astype(jnp.float32), 1.0, 0.0).astype(jnp.bfloat16)
    slots = jnp.concatenate([got_ref[s, block:, :] for s in range(sources)], axis=0)
    positive = jnp.dot(chosen, slots, preferred_element_type=jnp.float32)
    out_ref[:, :depth] = summed.astype(jnp.bfloat16)
    out_ref[:, depth:2 * depth] = positive.astype(jnp.bfloat16)
    hi, mid, low = split3(jnp.broadcast_to(turned[:, 2 * sources:2 * sources + 1], (block, LANES)))
    lane = iota((1, LANES), 1)
    zero = jnp.zeros((block, LANES), jnp.bfloat16)
    out_ref[:, 2 * depth:] = jnp.where(lane == 0, hi, jnp.where(lane == 1, mid, jnp.where(lane == 2, low, zero)))


def combine(got_ref, own_ref, positive, grad_ref, loss_ref):
    own, depth = own_ref.shape
    scale = 1.0 / math.sqrt(depth)
    logs = jnp.sum(got_ref[:, :, 2 * depth:].astype(jnp.float32), axis=2, keepdims=True)
    top = jnp.max(logs, axis=0, keepdims=True)
    share = jnp.exp2(logs - top)
    total = jnp.sum(share, axis=0)
    summed = jnp.sum(got_ref[:, :, :depth].astype(jnp.float32) * share, axis=0)
    grad_ref[...] = (summed / total - positive) * scale
    pos_score = jnp.sum(own_ref[...].astype(jnp.float32) * positive, axis=1, keepdims=True) * scale
    loss = (top[0] + jnp.log2(total)) * (1.0 / LOG2E) - pos_score
    line, lane = iota((own, LANES), 0), iota((own, LANES), 1)
    loss_ref[...] = jnp.sum(jnp.where(line == lane, loss, 0.0), axis=0)[:own]


def slots_kernel(got_ref, own_ref, grad_ref, loss_ref):
    depth = own_ref.shape[1]
    positive = jnp.sum(got_ref[:, :, depth:2 * depth].astype(jnp.float32), axis=0)
    combine(got_ref, own_ref, positive, grad_ref, loss_ref)


def rows_kernel(got_ref, own_ref, positive_ref, grad_ref, loss_ref):
    combine(got_ref, own_ref, positive_ref[...], grad_ref, loss_ref)


def routes(groups):
    plane, first_ring, second_ring = [], [], []
    for g in range(groups):
        table = [[g * SIDE * SIDE + z * SIDE + y for y in range(SIDE)] for z in range(SIDE)]
        turned = [list(column) for column in zip(*table)]
        if g % 2:
            table, turned = turned, table
        plane.append([device for row in table for device in row])
        first_ring += turned
        second_ring += table
    return plane, first_ring, second_ring


def per_device(queries, positives, cache, fresh, slots):
    own, depth = queries.shape
    rows = cache.shape[0]
    shards = lax.axis_size("shard")
    groups = lax.axis_size("group")
    count = shards * own
    every = ("group", "shard")
    plane, first_ring, second_ring = routes(groups)
    first = lax.axis_index("shard") * rows

    vmem = pl.BlockSpec(memory_space=pltpu.VMEM)
    smem = pl.BlockSpec(memory_space=pltpu.SMEM)
    start = first.reshape(1).astype(jnp.int32)
    wide = depth + LANES
    sent, new = pl.pallas_call(
        sent_kernel,
        out_shape=(
            jax.ShapeDtypeStruct((shards, own, wide), jnp.bfloat16),
            jax.ShapeDtypeStruct((fresh.shape[0], wide), jnp.bfloat16),
        ),
        in_specs=[smem, smem, smem, vmem, vmem], out_specs=(vmem, vmem),
    )(start, positives, slots, queries, fresh)
    got = lax.all_to_all(sent, every, 0, 0, axis_index_groups=plane).reshape(count, wide)
    pair = jnp.concatenate([new, lax.ppermute(new, "group", [(i, i ^ 1) for i in range(groups)])], axis=0)
    pieces = [pair] + [
        lax.ppermute(pair, "group", [(i, (i + 2 * k) % groups) for i in range(groups)])
        for k in range(1, groups // 2)
    ]
    extra = groups * fresh.shape[0]
    block = count // SIDE
    width = 2 * depth + LANES
    part, spill = pl.pallas_call(
        functools.partial(partial_kernel, CHUNK, shards),
        out_shape=(
            jax.ShapeDtypeStruct((SIDE, block + TAIL, depth), jnp.bfloat16),
            jax.ShapeDtypeStruct((1,), jnp.int32),
        ),
        in_specs=[smem, vmem] + [vmem] * len(pieces) + [pl.BlockSpec(memory_space=pl.ANY)],
        out_specs=(vmem, smem),
        scratch_shapes=[
            pltpu.VMEM((rows, depth), jnp.bfloat16),
            pltpu.VMEM((extra, wide), jnp.bfloat16),
            pltpu.VMEM((count, rows + extra), jnp.float32),
            pltpu.VMEM((count + PACKED, rows + extra), jnp.bfloat16),
            pltpu.SemaphoreType.DMA,
        ],
        compiler_params=pltpu.CompilerParams(vmem_limit_bytes=48 * 1024 * 1024),
        cost_estimate=pl.CostEstimate(
            flops=4 * count * rows * depth, bytes_accessed=2 * rows * depth, transcendentals=count * rows
        ),
    )(start, got, *pieces, cache)

    part = lax.all_to_all(part, every, 0, 0, axis_index_groups=first_ring)
    part = pl.pallas_call(
        block_kernel,
        out_shape=jax.ShapeDtypeStruct((block, width), jnp.bfloat16),
        in_specs=[vmem], out_specs=vmem,
        compiler_params=pltpu.CompilerParams(vmem_limit_bytes=32 * 1024 * 1024),
    )(part)
    back = lax.all_to_all(part.reshape(SIDE, own, width), every, 0, 0, axis_index_groups=second_ring)
    outs = (
        jax.ShapeDtypeStruct((own, depth), jnp.float32),
        jax.ShapeDtypeStruct((own,), jnp.float32),
    )
    params = pltpu.CompilerParams(vmem_limit_bytes=32 * 1024 * 1024)

    def from_slots():
        return pl.pallas_call(
            slots_kernel, out_shape=outs,
            in_specs=[vmem, vmem], out_specs=(vmem, vmem), compiler_params=params,
        )(back, queries)

    def from_rows():
        new = jnp.concatenate(pieces, axis=0)
        digits = got[:, depth:depth + 3].astype(jnp.int32)
        local = digits[:, 0] + 256 * digits[:, 1] + 65536 * digits[:, 2] - first
        at = new[:, depth:depth + 2].astype(jnp.int32)
        is_new = local[:, None] == (at[:, 0] + 256 * at[:, 1])[None, :]
        new_rows = jnp.dot(
            is_new.astype(jnp.bfloat16), new[:, :depth], preferred_element_type=jnp.float32
        ).astype(jnp.bfloat16)
        old_rows = cache[jnp.clip(local, 0, rows - 1)]
        owned = (local >= 0) & (local < rows)
        picked = jnp.where(jnp.any(is_new, axis=1)[:, None], new_rows, jnp.where(owned[:, None], old_rows, 0))
        picked = lax.all_to_all(picked.reshape(shards, own, depth), every, 0, 0, axis_index_groups=plane)
        positive = jnp.sum(picked.astype(jnp.float32), axis=0)
        return pl.pallas_call(
            rows_kernel, out_shape=outs,
            in_specs=[vmem, vmem, vmem], out_specs=(vmem, vmem), compiler_params=params,
        )(back, queries, positive)

    grad, loss = lax.cond(spill[0] > 0, from_rows, from_slots)
    return grad, loss


def solution(mesh):
    return jax.shard_map(
        per_device,
        mesh=mesh,
        in_specs=(
            P(("group", "shard"), None),
            P(("group", "shard")),
            P("shard", None),
            P(("group", "shard"), None),
            P(("group", "shard")),
        ),
        out_specs=(P(("group", "shard"), None), P(("group", "shard"))),
        check_vma=False,
    )
```

```python
import functools
import math

import jax
import jax.numpy as jnp
from jax import lax
from jax.experimental import pallas as pl
from jax.experimental.pallas import tpu as pltpu
from jax.sharding import PartitionSpec as P

LANES = 128
SIDE = 8
SLOTS = 12
TAIL = 16
CHUNK = 1024
PACKED = 64
LOG2E = math.log2(math.e)
NT = (((1,), (1,)), ((), ()))


def with_digits(numbers, rows, digits):
    line, lane = iota((len(numbers), LANES), 0), iota((len(numbers), LANES), 1)
    tail = jnp.zeros((len(numbers), LANES), jnp.float32)
    for n, number in enumerate(numbers):
        for k in range(digits):
            digit = ((number >> (8 * k)) & 255).astype(jnp.float32)
            tail = jnp.where((line == n) & (lane == k), digit, tail)
    return jnp.concatenate([rows, tail.astype(rows.dtype)], axis=1)


def sent_kernel(first_ref, pos_ref, slots_ref, queries_ref, fresh_ref, out_ref, new_ref):
    own, added = queries_ref.shape[0], fresh_ref.shape[0]
    whole = with_digits([pos_ref[n] for n in range(own)], queries_ref[...], 3)
    out_ref[...] = jnp.broadcast_to(whole[None], out_ref.shape)
    new_ref[...] = with_digits([slots_ref[n] - first_ref[0] for n in range(added)], fresh_ref[...], 2)


def split3(x):
    hi = x.astype(jnp.bfloat16)
    rest = x - hi.astype(jnp.float32)
    mid = rest.astype(jnp.bfloat16)
    low = (rest - mid.astype(jnp.float32)).astype(jnp.bfloat16)
    return hi, mid, low


def iota(shape, dim):
    return lax.broadcasted_iota(jnp.int32, shape, dim)


def as_row(digit_rows, digits):
    turned = digit_rows.astype(jnp.float32).T
    row = turned[0:1]
    for k in range(1, digits):
        row = row + turned[k:k + 1] * 256.0**k
    return row


def plan_positives(pos, first, rows, shards, sides):
    count = pos.shape[1]
    local = pos - first
    owned = (local >= 0.0) & (local < rows)
    holder = jnp.floor((pos + 0.5) * (1.0 / rows))
    lane = iota((1, count), 1)
    block = lane // (count // sides)
    order = jnp.where(owned, 1.0, 0.0)
    k = 1
    while k < count:
        order = order + jnp.where(lane >= k, pltpu.roll(order, k, 1), 0.0)
        k *= 2
    before = jnp.zeros((1, count), jnp.float32)
    held = jnp.zeros((shards, 1), jnp.float32)
    most = 0.0
    is_holder = jnp.where(holder == iota((shards, 1), 0).astype(jnp.float32), 1.0, 0.0)
    for b in range(sides):
        here = block == b
        earlier = jnp.max(jnp.where(block < b, order, 0.0))
        before = jnp.where(here, earlier, before)
        part = jnp.sum(jnp.where(here, is_holder, 0.0), axis=1, keepdims=True)
        most = jnp.maximum(most, jnp.max(part))
        held = held + part
    spill = (most > SLOTS) | (jnp.max(held) > PACKED)
    slot = jnp.where(owned, order - before, 0.0)
    place = jnp.where(slot <= SLOTS, (block * TAIL).astype(jnp.float32) + slot, 0.0)
    hit = owned & (order == iota((PACKED, 1), 0).astype(jnp.float32) + 1.0)
    column = jnp.sum(jnp.where(hit, local + 1.0, 0.0), axis=1, keepdims=True) - 1.0
    place = jnp.sum(jnp.where(hit, place, 0.0), axis=1, keepdims=True) - 1.0
    return column, place, slot, spill


def stage_kernel(cache_ref, other_ref, staged_ref, sem):
    copy = pltpu.make_async_copy(cache_ref.at[pl.ds(0, staged_ref.shape[0]), :], staged_ref, sem)
    copy.start()
    copy.wait()


def partial_kernel(chunk, shards, first_ref, got_ref, *refs):
    *new_refs, staged_ref, cache_ref, out_ref, spill_ref, table_ref, new_ref, scores_ref, both_ref, sem = refs
    count, width = got_ref.shape
    depth = width - LANES
    rows = cache_ref.shape[0]
    extra = new_ref.shape[0]
    to_log2 = LOG2E / math.sqrt(depth)
    load = pltpu.make_async_copy(cache_ref.at[pl.ds(chunk, rows - chunk), :], table_ref, sem)
    load.start()
    piece = extra // len(new_refs)
    for n, ref in enumerate(new_refs):
        new_ref[n * piece:(n + 1) * piece, :] = ref[...]
    pos = as_row(got_ref[:, depth:], 3)
    column, place, slot, spill = plan_positives(pos, first_ref[0].astype(jnp.float32), rows, shards, SIDE)
    spill_ref[0] = spill.astype(jnp.int32)

    new_digits = new_ref[:, depth:]
    new_row = as_row(new_digits, 2)
    weight = jnp.where(iota((1, LANES), 1) == 0, 1.0, jnp.where(iota((1, LANES), 1) == 1, 256.0, 0.0))
    new_column = jnp.sum(new_digits.astype(jnp.float32) * weight, axis=1, keepdims=True)

    spans = [(start, chunk) for start in range(0, rows, chunk)] + [(rows, extra)]

    def block_of(start, size):
        if start == rows:
            return new_ref[:, :depth]
        return staged_ref[...] if start == 0 else table_ref[start - chunk:start - chunk + size, :]

    names, dead = [], []
    for start, size in spans:
        name, gone = new_row, None
        if start < rows:
            name = (iota((1, size), 1) + start).astype(jnp.float32)
            gone = jnp.max(jnp.where(new_column == name, 1.0, 0.0), axis=0, keepdims=True) > 0.0
            name = jnp.where(gone, -2.0, name)
        names.append(name)
        dead.append(gone)
    for (start, size), name in zip(spans, names):
        both_ref[count:, start:start + size] = jnp.where(column == name, 1.0, 0.0).astype(jnp.bfloat16)

    blocks = [[spans[-1], spans[0]]] + [[span] for span in spans[1:-1]]
    order = dict(zip(spans, range(len(spans))))
    tops, totals, sums = [], [], []

    def score(g):
        top = jnp.full((count, LANES), -jnp.inf, jnp.float32)
        for span in blocks[g]:
            start, size = span
            part = lax.dot_general(
                got_ref[:, :depth], block_of(start, size), NT, preferred_element_type=jnp.float32
            )
            gone = dead[order[span]]
            if gone is not None:
                part = jnp.where(gone, -jnp.inf, part)
            scores_ref[:, start:start + size] = part
            for at in range(0, size, LANES):
                top = jnp.maximum(top, part[:, at:at + LANES])
        tops.append(jnp.max(top, axis=1, keepdims=True) * to_log2)

    def weigh(g):
        total = jnp.zeros((count, LANES), jnp.float32)
        for start, size in blocks[g]:
            weights = jnp.exp2(scores_ref[:, start:start + size] * to_log2 - tops[g])
            for at in range(0, size, LANES):
                total = total + weights[:, at:at + LANES]
            both_ref[:count, start:start + size] = weights.astype(jnp.bfloat16)
        totals.append(jnp.sum(total, axis=1, keepdims=True))

    def add(g):
        part = 0.0
        for start, size in blocks[g]:
            part = part + jnp.dot(
                both_ref[:, start:start + size], block_of(start, size), preferred_element_type=jnp.float32
            )
        sums.append(part)

    last = len(blocks)
    for g in range(last + 2):
        if g == 1:
            load.wait()
        if g < last:
            score(g)
        if 1 <= g <= last:
            weigh(g - 1)
        if g >= 2:
            add(g - 2)
    top = functools.reduce(jnp.maximum, tops)
    shares = [jnp.exp2(part - top) for part in tops]
    total = sum(part * share for part, share in zip(totals, shares))
    picked = sum(part[count:] for part in sums)
    summed = sum(part[:count] * share for part, share in zip(sums, shares))
    mean = (summed / total).astype(jnp.bfloat16)

    packed = picked.astype(jnp.bfloat16)
    place_row = jnp.broadcast_to(place, (PACKED, LANES)).T[0:1]
    spread = jnp.where(iota((SIDE * TAIL, 1), 0).astype(jnp.float32) == place_row, 1.0, 0.0).astype(jnp.bfloat16)
    spread = jnp.dot(spread, packed, preferred_element_type=jnp.float32)
    logs = jnp.broadcast_to(top + jnp.log2(total), (count, LANES)).T[0:1]
    facts = [part.astype(jnp.float32) for part in split3(logs)] + [slot]
    block = count // SIDE
    line, lane = iota((TAIL, LANES), 0), iota((TAIL, LANES), 1)
    for b in range(SIDE):
        at = b * block // LANES * LANES
        tail = spread[b * TAIL:(b + 1) * TAIL]
        first_tile = tail[:, :LANES]
        for k, fact in enumerate(facts):
            piece = fact[:, at:at + LANES]
            if b * block % LANES:
                piece = pltpu.roll(piece, LANES - b * block % LANES, 1)
            first_tile = jnp.where((line == SLOTS + k) & (lane < block), piece, first_tile)
        out_ref[b, :block, :] = mean[b * block:(b + 1) * block]
        out_ref[b, block:, :LANES] = first_tile.astype(jnp.bfloat16)
        out_ref[b, block:, LANES:] = tail[:, LANES:].astype(jnp.bfloat16)


def block_kernel(got_ref, out_ref):
    sources, lines, depth = got_ref.shape
    block = lines - TAIL
    source = iota((sources, LANES), 0)
    logs = jnp.zeros((sources, LANES), jnp.float32)
    slot = jnp.zeros((sources, LANES), jnp.float32)
    for s in range(sources):
        tail = got_ref[s, block:, :LANES].astype(jnp.float32)
        log = tail[SLOTS:SLOTS + 1] + tail[SLOTS + 1:SLOTS + 2] + tail[SLOTS + 2:SLOTS + 3]
        logs = jnp.where(source == s, log, logs)
        slot = jnp.where(source == s, tail[SLOTS + 3:SLOTS + 4], slot)
    top = jnp.max(logs, axis=0, keepdims=True)
    share = jnp.exp2(logs - top)
    total = jnp.sum(share, axis=0, keepdims=True)
    share = share / total
    whole = jnp.broadcast_to(top + jnp.log2(total), (sources, LANES))
    rest = jnp.zeros((LANES - 3 * sources, LANES), jnp.float32)
    turned = jnp.concatenate([share, slot, whole, rest], axis=0).T[:block]

    summed = jnp.zeros((block, depth), jnp.float32)
    for s in range(sources):
        summed = summed + got_ref[s, :block, :].astype(jnp.float32) * turned[:, s:s + 1]
    lane = iota((1, sources * TAIL), 1)
    wanted = jnp.zeros((block, sources * TAIL), jnp.float32)
    for s in range(sources):
        wanted = jnp.where(lane // TAIL == s, turned[:, sources + s:sources + s + 1], wanted)
    chosen = jnp.where(wanted == (lane % TAIL + 1).astype(jnp.float32), 1.0, 0.0).astype(jnp.bfloat16)
    slots = jnp.concatenate([got_ref[s, block:, :] for s in range(sources)], axis=0)
    positive = jnp.dot(chosen, slots, preferred_element_type=jnp.float32)
    out_ref[:, :depth] = summed.astype(jnp.bfloat16)
    out_ref[:, depth:2 * depth] = positive.astype(jnp.bfloat16)
    hi, mid, low = split3(jnp.broadcast_to(turned[:, 2 * sources:2 * sources + 1], (block, LANES)))
    lane = iota((1, LANES), 1)
    zero = jnp.zeros((block, LANES), jnp.bfloat16)
    out_ref[:, 2 * depth:] = jnp.where(lane == 0, hi, jnp.where(lane == 1, mid, jnp.where(lane == 2, low, zero)))


def combine(got_ref, own_ref, positive, grad_ref, loss_ref):
    own, depth = own_ref.shape
    scale = 1.0 / math.sqrt(depth)
    logs = jnp.sum(got_ref[:, :, 2 * depth:].astype(jnp.float32), axis=2, keepdims=True)
    top = jnp.max(logs, axis=0, keepdims=True)
    share = jnp.exp2(logs - top)
    total = jnp.sum(share, axis=0)
    summed = jnp.sum(got_ref[:, :, :depth].astype(jnp.float32) * share, axis=0)
    grad_ref[...] = (summed / total - positive) * scale
    pos_score = jnp.sum(own_ref[...].astype(jnp.float32) * positive, axis=1, keepdims=True) * scale
    loss = (top[0] + jnp.log2(total)) * (1.0 / LOG2E) - pos_score
    line, lane = iota((own, LANES), 0), iota((own, LANES), 1)
    loss_ref[...] = jnp.sum(jnp.where(line == lane, loss, 0.0), axis=0)[:own]


def slots_kernel(got_ref, own_ref, grad_ref, loss_ref):
    depth = own_ref.shape[1]
    positive = jnp.sum(got_ref[:, :, depth:2 * depth].astype(jnp.float32), axis=0)
    combine(got_ref, own_ref, positive, grad_ref, loss_ref)


def rows_kernel(got_ref, own_ref, positive_ref, grad_ref, loss_ref):
    combine(got_ref, own_ref, positive_ref[...], grad_ref, loss_ref)


def routes(groups):
    plane, first_ring, second_ring = [], [], []
    for g in range(groups):
        table = [[g * SIDE * SIDE + z * SIDE + y for y in range(SIDE)] for z in range(SIDE)]
        turned = [list(column) for column in zip(*table)]
        if g % 2:
            table, turned = turned, table
        plane.append([device for row in table for device in row])
        first_ring += turned
        second_ring += table
    return plane, first_ring, second_ring


def per_device(queries, positives, cache, fresh, slots):
    own, depth = queries.shape
    rows = cache.shape[0]
    shards = lax.axis_size("shard")
    groups = lax.axis_size("group")
    count = shards * own
    every = ("group", "shard")
    plane, first_ring, second_ring = routes(groups)
    first = lax.axis_index("shard") * rows

    vmem = pl.BlockSpec(memory_space=pltpu.VMEM)
    smem = pl.BlockSpec(memory_space=pltpu.SMEM)
    start = first.reshape(1).astype(jnp.int32)
    wide = depth + LANES
    sent, new = pl.pallas_call(
        sent_kernel,
        out_shape=(
            jax.ShapeDtypeStruct((shards, own, wide), jnp.bfloat16),
            jax.ShapeDtypeStruct((fresh.shape[0], wide), jnp.bfloat16),
        ),
        in_specs=[smem, smem, smem, vmem, vmem], out_specs=(vmem, vmem),
    )(start, positives, slots, queries, fresh)
    got = lax.all_to_all(sent, every, 0, 0, axis_index_groups=plane).reshape(count, wide)
    pair = jnp.concatenate([new, lax.ppermute(new, "group", [(i, i ^ 1) for i in range(groups)])], axis=0)
    pieces = [pair] + [
        lax.ppermute(pair, "group", [(i, (i + 2 * k) % groups) for i in range(groups)])
        for k in range(1, groups // 2)
    ]
    anywhere = pl.BlockSpec(memory_space=pl.ANY)
    staged = pl.pallas_call(
        stage_kernel,
        out_shape=pltpu.VMEM((CHUNK, depth), jnp.bfloat16),
        in_specs=[anywhere, anywhere], out_specs=vmem,
        scratch_shapes=[pltpu.SemaphoreType.DMA],
        compiler_params=pltpu.CompilerParams(vmem_limit_bytes=2 * 1024 * 1024),
    )(cache, pieces[-1])
    extra = groups * fresh.shape[0]
    block = count // SIDE
    width = 2 * depth + LANES
    part, spill = pl.pallas_call(
        functools.partial(partial_kernel, CHUNK, shards),
        out_shape=(
            jax.ShapeDtypeStruct((SIDE, block + TAIL, depth), jnp.bfloat16),
            jax.ShapeDtypeStruct((1,), jnp.int32),
        ),
        in_specs=[smem, vmem] + [vmem] * (len(pieces) + 1) + [anywhere],
        out_specs=(vmem, smem),
        scratch_shapes=[
            pltpu.VMEM((rows - CHUNK, depth), jnp.bfloat16),
            pltpu.VMEM((extra, wide), jnp.bfloat16),
            pltpu.VMEM((count, rows + extra), jnp.float32),
            pltpu.VMEM((count + PACKED, rows + extra), jnp.bfloat16),
            pltpu.SemaphoreType.DMA,
        ],
        compiler_params=pltpu.CompilerParams(vmem_limit_bytes=48 * 1024 * 1024),
        cost_estimate=pl.CostEstimate(
            flops=4 * count * rows * depth, bytes_accessed=2 * rows * depth, transcendentals=count * rows
        ),
    )(start, got, *pieces, staged, cache)

    part = lax.all_to_all(part, every, 0, 0, axis_index_groups=first_ring)
    part = pl.pallas_call(
        block_kernel,
        out_shape=jax.ShapeDtypeStruct((block, width), jnp.bfloat16),
        in_specs=[vmem], out_specs=vmem,
        compiler_params=pltpu.CompilerParams(vmem_limit_bytes=32 * 1024 * 1024),
    )(part)
    back = lax.all_to_all(part.reshape(SIDE, own, width), every, 0, 0, axis_index_groups=second_ring)
    outs = (
        jax.ShapeDtypeStruct((own, depth), jnp.float32),
        jax.ShapeDtypeStruct((own,), jnp.float32),
    )
    params = pltpu.CompilerParams(vmem_limit_bytes=32 * 1024 * 1024)

    def from_slots():
        return pl.pallas_call(
            slots_kernel, out_shape=outs,
            in_specs=[vmem, vmem], out_specs=(vmem, vmem), compiler_params=params,
        )(back, queries)

    def from_rows():
        new = jnp.concatenate(pieces, axis=0)
        digits = got[:, depth:depth + 3].astype(jnp.int32)
        local = digits[:, 0] + 256 * digits[:, 1] + 65536 * digits[:, 2] - first
        at = new[:, depth:depth + 2].astype(jnp.int32)
        is_new = local[:, None] == (at[:, 0] + 256 * at[:, 1])[None, :]
        new_rows = jnp.dot(
            is_new.astype(jnp.bfloat16), new[:, :depth], preferred_element_type=jnp.float32
        ).astype(jnp.bfloat16)
        old_rows = cache[jnp.clip(local, 0, rows - 1)]
        owned = (local >= 0) & (local < rows)
        picked = jnp.where(jnp.any(is_new, axis=1)[:, None], new_rows, jnp.where(owned[:, None], old_rows, 0))
        picked = lax.all_to_all(picked.reshape(shards, own, depth), every, 0, 0, axis_index_groups=plane)
        positive = jnp.sum(picked.astype(jnp.float32), axis=0)
        return pl.pallas_call(
            rows_kernel, out_shape=outs,
            in_specs=[vmem, vmem, vmem], out_specs=(vmem, vmem), compiler_params=params,
        )(back, queries, positive)

    grad, loss = lax.cond(spill[0] > 0, from_rows, from_slots)
    return grad, loss


def solution(mesh):
    return jax.shard_map(
        per_device,
        mesh=mesh,
        in_specs=(
            P(("group", "shard"), None),
            P(("group", "shard")),
            P("shard", None),
            P(("group", "shard"), None),
            P(("group", "shard")),
        ),
        out_specs=(P(("group", "shard"), None), P(("group", "shard"))),
        check_vma=False,
    )
```
